32 devices in a mesh: head: 4 (over y, core), expert: 8 (over z, x).
Axes of the slice: x: 2, y: 2, z: 4, core: 2. Of those that a mesh axis runs over, the one named last changes fastest.
Arguments:
- attention: bfloat16 [1024, 6144], P('expert', 'head'), may hold values from -6 to 6
- out_proj: bfloat16 [6144, 6144], P('head', 'expert'), may hold values from -0.078125 to 0.078125
- residual: bfloat16 [1024, 6144], P('expert', 'head'), may hold values from -64 to 64
- norm_gain: bfloat16 [6144], P('head'), may hold values from 0.25 to 1.75
- router: float32 [6144, 4], P('head'), may hold values from -0.02734375 to 0.02734375
- routes: int32 [1024, 2], P('expert'), may hold values from 0 to 3, all different within a row; in each aligned block of 128 rows (0 to 127, 128 to 255, ...) at most 72 rows name the same one
- cotangent: bfloat16 [1024, 6144], P('expert', 'head'), may hold values from -4 to 4
- gate_weight: bfloat16 [8, 6144, 4096], P('expert', None, 'head'), may hold values from -0.078125 to 0.078125
- up_weight: bfloat16 [8, 6144, 4096], P('expert', None, 'head'), may hold values from -0.078125 to 0.078125
- down_weight: bfloat16 [8, 4096, 6144], P('expert', None, 'head'), may hold values from -0.0625 to 0.0625
Outputs:
- layer_out: float32 [1024, 6144], P('expert', 'head')
- grad_gate: bfloat16 [8, 6144, 4096], P('expert', None, 'head')
- grad_up: bfloat16 [8, 6144, 4096], P('expert', None, 'head')
- grad_down: bfloat16 [8, 4096, 6144], P('expert', None, 'head')
The draws below stay inside these ranges and needn't reach their ends.
Inputs may be any that keep to these rules, and one draw needn't show every extreme that they name: `routes`: each row names two different experts. In each aligned block of 128 rows (the rows of one index of expert) no expert is named by more than 72 rows, and in some block one expert is named by exactly 72 rows.
All inputs are finite; a program needn't handle non-finite values.
Results may differ from the reference program's by a relative error of at most 0.025.
Values may be sent and summed in bfloat16 or wider, within the bound.
No kernel may reach another device: no remote copies, remote signals or barrier semaphores. Data moves between devices by JAX's collectives and lax.ppermute only.
A program may use at most 192 MiB of HBM per device.

```python
import math
import jax
import jax.numpy as jnp
import numpy as np
from jax import lax

D = 6144
HEADS = 48
HEAD_DIM = 128
FF = 8192
EXPERTS = 4
TOK_DEV = 128
TOKENS = 1024
CAP = 72
GROUP = 2
FFG = 4096
N_HEAD = 4
N_EXPERT = 8


def draw_residual(key, part):
    key_base, key_rows, key_cols = jax.random.split(key, 3)
    column = jnp.arange(D, dtype=jnp.float32) / D
    base = jnp.clip(jax.random.normal(key_base, (TOKENS, D), jnp.float32), -6.0, 6.0)
    rising = jnp.sqrt(1.0 + 2.0 * column)
    row_scale = jnp.exp(jax.random.uniform(key_rows, (TOKENS, 1), jnp.float32, -1.6, 0.7))
    col_scale = jnp.exp(jax.random.uniform(key_cols, (1, D), jnp.float32, -0.7, 0.7))
    return (base * row_scale * col_scale * rising[None, :]).astype(jnp.bfloat16)


def levels(key, dims, cuts, least, largest):
    level, own = 1.0, jax.random.fold_in(key, 6)
    for dim, shards_of in cuts:
        draws = jnp.exp(jax.random.uniform(jax.random.fold_in(own, dim), (shards_of,), jnp.float32, least / len(cuts), largest / len(cuts)))
        level = level * jnp.repeat(draws, dims[dim] // shards_of).reshape([-1 if axis == dim else 1 for axis in range(len(dims))])
    return level


def deal_out(own_key, own, number, rows, count, top, reach, slope):
    order = jax.random.permutation(own_key, count)
    heavy_load, ordinary = load_shares(count, rows * top, reach, slope, True), load_shares(count, rows * top, reach, slope, False)
    places = jnp.arange(count)

    def named(lengths, offset_by):
        used = int((lengths > 0).sum())
        fixed = max(1, used // 4)
        passed = fixed + (places - fixed + offset_by * (used - fixed)) % max(1, count - fixed)
        return jnp.zeros((count,), jnp.int32).at[order[jnp.where(places < fixed, places, passed)]].set(jnp.asarray(lengths, jnp.int32))

    lengths = jnp.where(number % 4 == 0, named(heavy_load, number // 4), named(ordinary, number - number // 4 - 1))
    mixed = jax.random.permutation(jax.random.fold_in(own, 3), count)
    source_of, sink = mixed[0:count // 2 * 2:2], mixed[1:count // 2 * 2:2]
    margin = jnp.minimum(lengths[source_of] - 1, reach - lengths[sink]) // 2
    margin = jnp.where((source_of == order[0]) | (sink == order[0]) | (lengths[sink] == 0), 0, jnp.maximum(margin, 0))
    passed = jax.random.randint(jax.random.fold_in(own, 4), (count // 2,), 0, 1 << 20) % (margin + 1)
    lengths = lengths.at[source_of].add(-passed).at[sink].add(passed)
    items = jnp.searchsorted(jnp.cumsum(lengths), jnp.arange(rows * top), side="right").astype(jnp.int32)
    table = items.reshape(top, rows).T
    table = table[jax.random.permutation(jax.random.fold_in(own, 1), rows)]
    offset_by = jax.random.randint(jax.random.fold_in(own, 2), (rows, 1), 0, top)
    return jnp.take_along_axis(table, (jnp.arange(top)[None, :] + offset_by) % top, axis=1)


def load_shares(number_of, total, most, lean, full):
    loads = [(1 << 20) // math.isqrt(grade ** lean) + 1 for grade in range(1, number_of + 1)]
    largest = most if full else min(most, max(-(-total // number_of), total * loads[0] // sum(loads)))
    least = 1 if total - largest >= number_of - 1 else 0
    holding, surplus = [largest] + [least] * (number_of - 1), total - largest - least * (number_of - 1)
    while surplus > 0:
        movable = [i for i in range(1, number_of) if holding[i] < largest] or [i for i in range(1, number_of) if holding[i] < most]
        mass, budget = sum([loads[i] for i in movable]), surplus
        for i in movable:
            addition = min(most - holding[i], max(1, budget * loads[i] // mass), surplus)
            holding[i] = holding[i] + addition
            surplus = surplus - addition
    return np.array(holding)


def bell_draw(own_key, extent, scale, bound, cuts=(), kind=jnp.bfloat16):
    level = levels(own_key, extent, cuts, -0.22, 0.18) if cuts else 1.0
    values = jax.random.normal(own_key, extent, jnp.float32) * scale * level
    return jnp.minimum(jnp.maximum(values, -bound), bound).astype(kind)


def setup_inputs(seed: int = 0) -> dict:
    key_of = jax.random.split(jax.random.key(seed), 11)
    attention = bell_draw(key_of[0], (TOKENS, HEADS * HEAD_DIM), 1.0, 6.0, ((0, 8), (1, 4)))
    out_proj = bell_draw(key_of[1], (HEADS * HEAD_DIM, D), (HEADS * HEAD_DIM) ** -0.5, 0.078125, ((0, 4), (1, 8)))
    residual = draw_residual(jax.random.fold_in(key_of[10], 71), 0)
    norm_gain = jnp.clip(1.0 + 0.15 * jax.random.normal(key_of[3], (D,), jnp.float32), 0.25, 1.75).astype(jnp.bfloat16)
    router = bell_draw(key_of[4], (D, EXPERTS), (8 * D) ** -0.5, 0.02734375, ((0, 4),), jnp.float32)
    routes_keys = jax.random.split(jax.random.fold_in(key_of[5], 1), TOKENS // TOK_DEV)
    routes_turns = jax.random.permutation(jax.random.fold_in(key_of[5], 3), TOKENS // TOK_DEV)
    routes = jax.vmap(lambda own, number: deal_out(jax.random.fold_in(key_of[5], 2), own, number, TOK_DEV, EXPERTS, 2, CAP, 2))(routes_keys, routes_turns).reshape((TOKENS, 2))
    cotangent = bell_draw(key_of[6], (TOKENS, D), 0.25, 4.0, ((0, 8), (1, 4)))
    gate_weight = bell_draw(key_of[7], (N_EXPERT, D, FFG), D ** -0.5, 0.078125, ((0, 8), (2, 4)))
    up_weight = bell_draw(key_of[8], (N_EXPERT, D, FFG), D ** -0.5, 0.078125, ((0, 8), (2, 4)))
    down_weight = bell_draw(key_of[9], (N_EXPERT, FFG, D), FF ** -0.5, 0.0625, ((0, 8), (2, 4)))
    return dict(attention=attention, out_proj=out_proj, residual=residual, norm_gain=norm_gain, router=router, routes=routes, cotangent=cotangent, gate_weight=gate_weight, up_weight=up_weight, down_weight=down_weight)


EPSILON = 1e-05

def reference(attention, out_proj, residual, norm_gain, router, routes, cotangent, gate_weight, up_weight, down_weight):
    proj = jnp.dot(attention, out_proj, preferred_element_type=jnp.float32)
    state = residual.astype(jnp.float32) + proj
    scaled = state * norm_gain.astype(jnp.float32)
    inverse = lax.rsqrt(lax.optimization_barrier(jnp.mean(state * state, axis=1, keepdims=True)) + EPSILON)
    normed = (scaled * inverse).astype(jnp.bfloat16)
    logits = inverse * jnp.dot(scaled, router, precision=lax.Precision.HIGHEST, preferred_element_type=jnp.float32)
    expert_ids = jnp.arange(EXPERTS, dtype=jnp.int32)
    first_id = routes[:, 0]
    second = routes[:, 1]
    logit_first = lax.optimization_barrier(jnp.sum(jnp.where(first_id[:, None] == expert_ids[None, :], logits, 0.0), axis=1, keepdims=True))
    logit_second = lax.optimization_barrier(jnp.sum(jnp.where(second[:, None] == expert_ids[None, :], logits, 0.0), axis=1, keepdims=True))
    prob_first = jax.nn.sigmoid(logit_first - logit_second)
    prob_second = jax.nn.sigmoid(logit_second - logit_first)
    hit_table = (routes.reshape(N_EXPERT, TOK_DEV * 2)[:, :, None] == expert_ids[None, None, :]).astype(jnp.int32)
    earlier = jnp.cumsum(hit_table, axis=1, dtype=jnp.int32) - hit_table
    slot_pair = lax.optimization_barrier(jnp.sum(earlier * hit_table, axis=2, dtype=jnp.int32)).reshape(TOKENS, 2)
    source = (jnp.arange(TOKENS, dtype=jnp.int32) // TOK_DEV).astype(jnp.int32)
    position = (source[:, None] * CAP + slot_pair).astype(jnp.int32)
    rows_total = N_EXPERT * CAP
    cot_first = (prob_first * cotangent.astype(jnp.float32)).astype(jnp.bfloat16)
    cot_second = (prob_second * cotangent.astype(jnp.float32)).astype(jnp.bfloat16)
    feature_block = D // N_HEAD
    contract_rows = (((0,), (0,)), ((), ()))
    output = state
    gate_list = []
    up_list = []
    down_list = []
    for expert in range(EXPERTS):
        is_first = first_id == expert
        is_second = second == expert
        index_first = jnp.where(is_first, position[:, 0], rows_total).astype(jnp.int32)
        index_second = jnp.where(is_second, position[:, 1], rows_total).astype(jnp.int32)
        x_rows = jnp.zeros((rows_total, D), jnp.bfloat16).at[index_first].set(normed, mode='drop').at[index_second].set(normed, mode='drop')
        cot_rows = jnp.zeros((rows_total, D), jnp.bfloat16).at[index_first].set(cot_first, mode='drop').at[index_second].set(cot_second, mode='drop')
        gate_w = jnp.transpose(gate_weight[expert * GROUP:(expert + 1) * GROUP], (1, 0, 2)).reshape(D, FF)
        up_w = jnp.transpose(up_weight[expert * GROUP:(expert + 1) * GROUP], (1, 0, 2)).reshape(D, FF)
        down_w = down_weight[expert * GROUP:(expert + 1) * GROUP].reshape(FF, D)
        gate_val = jnp.dot(x_rows, gate_w, preferred_element_type=jnp.float32)
        up_val = jnp.dot(x_rows, up_w, preferred_element_type=jnp.float32)
        act_gate = jax.nn.silu(gate_val)
        hidden = (act_gate * up_val).astype(jnp.bfloat16)
        out_rows = jnp.dot(hidden, down_w, preferred_element_type=jnp.float32).astype(jnp.bfloat16)
        took_first = jnp.take(out_rows, jnp.minimum(index_first, rows_total - 1), axis=0).astype(jnp.float32)
        took_second = jnp.take(out_rows, jnp.minimum(index_second, rows_total - 1), axis=0).astype(jnp.float32)
        output = output + jnp.where(is_first[:, None], prob_first * took_first, 0.0)
        output = output + jnp.where(is_second[:, None], prob_second * took_second, 0.0)
        grad_down_e = lax.dot_general(hidden, cot_rows, contract_rows, preferred_element_type=jnp.float32).astype(jnp.bfloat16)
        hidden_grad = jnp.zeros((rows_total, FF), jnp.float32)
        for block in range(N_HEAD):
            cot_cols = cot_rows[:, block * feature_block:(block + 1) * feature_block]
            down_cols = down_w[:, block * feature_block:(block + 1) * feature_block]
            term = lax.dot_general(cot_cols, down_cols, (((1,), (1,)), ((), ())), preferred_element_type=jnp.float32).astype(jnp.bfloat16)
            term = lax.optimization_barrier(term)
            hidden_grad = hidden_grad + term.astype(jnp.float32)
        gate_sigmoid = jax.nn.sigmoid(gate_val)
        gate_grad = (hidden_grad * up_val * gate_sigmoid * (1.0 + gate_val * (1.0 - gate_sigmoid))).astype(jnp.bfloat16)
        up_grad = (hidden_grad * act_gate).astype(jnp.bfloat16)
        grad_gate_e = lax.dot_general(x_rows, gate_grad, contract_rows, preferred_element_type=jnp.float32).astype(jnp.bfloat16)
        grad_up_e = lax.dot_general(x_rows, up_grad, contract_rows, preferred_element_type=jnp.float32).astype(jnp.bfloat16)
        gate_list.append(jnp.transpose(grad_gate_e.reshape(D, GROUP, FFG), (1, 0, 2)))
        up_list.append(jnp.transpose(grad_up_e.reshape(D, GROUP, FFG), (1, 0, 2)))
        down_list.append(grad_down_e.reshape(GROUP, FFG, D))
    return (output, jnp.concatenate(gate_list, axis=0), jnp.concatenate(up_list, axis=0), jnp.concatenate(down_list, axis=0))
```

```python
import functools

import jax
import jax.numpy as jnp
from jax import lax
from jax.experimental import pallas as pl
from jax.experimental.pallas import tpu as pltpu
from jax.sharding import Mesh, PartitionSpec as P

EPSILON = 1e-05
EXPERTS = 4
CORES = 2
LANES = 128
VMEM = 50 * 2**20
BF = jnp.bfloat16
F32 = jnp.float32
ALL_AXES = ("y", "c", "z", "x")


def shift(value, axis, step=1):
    size = lax.axis_size(axis)
    return lax.ppermute(value, axis, [(i, (i + step) % size) for i in range(size)])


def pick(stack, index, axis=0):
    return lax.dynamic_index_in_dim(stack, index, axis, keepdims=False)


def tie(*values):
    return lax.optimization_barrier(values)


def swap_pairs(n_y, n_z, n_x, parts, turn):
    pairs = []
    for y in range(n_y):
        for c in range(CORES):
            for z in range(n_z):
                for x in range(n_x):
                    piece = (y * CORES + c) * parts + (turn + z) % parts
                    to_z, to_c = piece // CORES, piece % CORES
                    to_y = z // parts
                    source = ((y * CORES + c) * n_z + z) * n_x + x
                    target = ((to_y * CORES + to_c) * n_z + to_z) * n_x + x
                    pairs.append((source, target))
    return pairs


def dot32(a, b, dims):
    return lax.dot_general(a, b, (dims, ((), ())), preferred_element_type=F32)


def sigmoid(value):
    return 1.0 / (1.0 + jnp.exp(-value))


def order(mine, other, index):
    first = index == 0
    return jnp.where(first, mine, other), jnp.where(first, other, mine)


def place_copies(plan, refs, scratch, sems):
    copies = []
    for number, (ref, lead, row, col) in enumerate(plan):
        source = refs[ref] if lead is None else refs[ref].at[lead]
        n_rows, n_cols = source.shape
        row = pl.multiple_of(row(), 16) if callable(row) else row
        col = pl.multiple_of(col(), LANES) if callable(col) else col
        copies.append(
            pltpu.make_async_copy(
                source,
                scratch.at[pl.ds(row, n_rows), pl.ds(col, n_cols)],
                sems.at[number],
            )
        )
    return copies


def whole(shape):
    return pl.BlockSpec(shape, lambda *_: (0,) * len(shape))


def column_tile(cols):
    return 256 if cols % 256 == 0 else cols


def params():
    return pltpu.CompilerParams(vmem_limit_bytes=VMEM)


def cost(flops, bytes_accessed, transcendentals=0):
    return pl.CostEstimate(
        flops=flops, bytes_accessed=bytes_accessed, transcendentals=transcendentals
    )


def forward_kernel(plan, n_refs, width, *args):
    refs = args[:n_refs]
    gate_w, up_w, stats, meta, hid, a_out, b_out, scale, x_out = args[n_refs:-5]
    x_all, inv, prob, sems, sem = args[-5:]
    step = pl.program_id(0)
    rows = x_all.shape[0]
    keep = pltpu.make_async_copy(x_all, x_out, sem)

    @pl.when(step == 0)
    def _():
        copies = place_copies(plan, refs, x_all, sems)
        for copy in copies:
            copy.start()
        for copy in copies:
            copy.wait()
        keep.start()
        raw = stats[...]
        mean = raw[:, LANES - 1 :] / width
        inv[...] = jnp.broadcast_to(lax.rsqrt(mean + EPSILON), (rows, LANES))
        lane = lax.broadcasted_iota(jnp.int32, (rows, LANES), 1)
        own = lax.axis_index("z")
        other = meta[...].astype(F32).astype(jnp.int32) - own
        expert = lane % EXPERTS
        sign = (expert == own).astype(F32) - (expert == other).astype(F32)
        sign = jnp.where(lane < 3 * EXPERTS, sign, 0.0)
        gap = jnp.sum(raw * sign, axis=1, keepdims=True) * inv[...]
        prob[...] = sigmoid(gap)
        scale[...] = prob[...] * inv[...]

    x = x_all[...]
    a = jnp.dot(x, gate_w[...], preferred_element_type=F32)
    b = jnp.dot(x, up_w[...], preferred_element_type=F32)
    inverse = inv[:, :1]
    a = a * inverse
    b = b * inverse
    hid[...] = (a * sigmoid(a) * b * prob[:, :1]).astype(BF)
    a_out[...] = a
    b_out[...] = b

    @pl.when(step == pl.num_programs(0) - 1)
    def _():
        keep.wait()


def forward(pieces, plan, gate_w, up_w, stats, meta, meta_block):
    width, cols = gate_w.shape
    rows = meta.shape[0]
    tile = 256 if cols % 256 == 0 else cols
    anywhere = pl.BlockSpec(memory_space=pl.ANY)
    return pl.pallas_call(
        functools.partial(forward_kernel, plan, len(pieces), width),
        grid=(cols // tile,),
        in_specs=[anywhere] * len(pieces)
        + [
            pl.BlockSpec((width, tile), lambda j: (0, j)),
            pl.BlockSpec((width, tile), lambda j: (0, j)),
            whole((rows, LANES)),
            pl.BlockSpec((rows, LANES), lambda j: (0, meta_block)),
        ],
        out_specs=[
            pl.BlockSpec((rows, tile), lambda j: (0, j)),
            pl.BlockSpec((rows, tile), lambda j: (0, j)),
            pl.BlockSpec((rows, tile), lambda j: (0, j)),
            whole((rows, LANES)),
            anywhere,
        ],
        out_shape=[
            jax.ShapeDtypeStruct((rows, cols), BF),
            jax.ShapeDtypeStruct((rows, cols), F32),
            jax.ShapeDtypeStruct((rows, cols), F32),
            jax.ShapeDtypeStruct((rows, LANES), F32),
            jax.ShapeDtypeStruct((rows, width), BF),
        ],
        scratch_shapes=[
            pltpu.VMEM((rows, width), BF),
            pltpu.VMEM((rows, LANES), F32),
            pltpu.VMEM((rows, LANES), F32),
            pltpu.SemaphoreType.DMA((len(plan),)),
            pltpu.SemaphoreType.DMA,
        ],
        compiler_params=pltpu.CompilerParams(vmem_limit_bytes=VMEM),
        cost_estimate=pl.CostEstimate(
            flops=4 * rows * width * cols,
            bytes_accessed=4 * width * cols + 2 * rows * width,
            transcendentals=rows * cols,
        ),
    )(*pieces, gate_w, up_w, stats, meta)


def gate_up_kernel(x, a_in, b_in, dh, scale, gate_out, up_out, da, db):
    @pl.when(pl.program_id(0) == 0)
    def _():
        cols = a_in.shape[1]
        for k in range(cols // LANES):
            at = slice(k * LANES, (k + 1) * LANES)
            a, b = a_in[:, at], b_in[:, at]
            s = sigmoid(a)
            grad = dh[:, at].astype(F32) * scale[...]
            da[:, at] = (grad * b * s * (1.0 + a * (1.0 - s))).astype(BF)
            db[:, at] = (grad * a * s).astype(BF)

    gate_out[...] = dot32(x[...], da[...], ((0,), (0,))).astype(BF)
    up_out[...] = dot32(x[...], db[...], ((0,), (0,))).astype(BF)


def gate_up_grads(x_rows, a, b, dh, scale):
    rows, width = x_rows.shape
    cols = a.shape[1]
    tile = 512
    out = pl.BlockSpec((tile, cols), lambda j: (j, 0))
    return pl.pallas_call(
        gate_up_kernel,
        grid=(width // tile,),
        in_specs=[
            pl.BlockSpec((rows, tile), lambda j: (0, j)),
            whole((rows, cols)),
            whole((rows, cols)),
            whole((rows, cols)),
            whole((rows, LANES)),
        ],
        out_specs=[out, out],
        out_shape=[jax.ShapeDtypeStruct((width, cols), BF)] * 2,
        scratch_shapes=[pltpu.VMEM((rows, cols), BF)] * 2,
        compiler_params=pltpu.CompilerParams(vmem_limit_bytes=VMEM),
        cost_estimate=pl.CostEstimate(
            flops=4 * rows * width * cols,
            bytes_accessed=4 * width * cols + 2 * rows * width + 10 * rows * cols,
            transcendentals=rows * cols,
        ),
    )(x_rows, a, b, dh, scale)


def down_store(value, out, split_rows):
    if split_rows is None:
        out[...] = value
        return
    n_y, n_x, size = split_rows
    for y in range(n_y):
        for x in range(n_x):
            at = (y * n_x + x) * size
            out[x, y * size : (y + 1) * size, :] = value[at : at + size]


def down_kernel(plan, n_refs, split_rows, *args):
    refs = args[:n_refs]
    down_w, out, hid_out, hid, sems, sem = args[n_refs:]
    step = pl.program_id(0)
    keep = pltpu.make_async_copy(hid, hid_out, sem)

    @pl.when(step == 0)
    def _():
        copies = place_copies(plan, refs, hid, sems)
        for copy in copies:
            copy.start()
        for copy in copies:
            copy.wait()
        keep.start()

    value = jnp.dot(hid[...], down_w[...], preferred_element_type=F32).astype(BF)
    down_store(value, out, split_rows)

    @pl.when(step == pl.num_programs(0) - 1)
    def _():
        keep.wait()


def down_next_kernel(split_rows, hid, down_w, out):
    value = jnp.dot(hid[...], down_w[...], preferred_element_type=F32).astype(BF)
    down_store(value, out, split_rows)


def down_specs(rows, hidden, tile, feats, base, split_rows):
    weight = pl.BlockSpec((hidden, tile), lambda j: (0, j + base))
    if split_rows is None:
        out = pl.BlockSpec((rows, tile), lambda j: (0, j))
        shape = jax.ShapeDtypeStruct((rows, feats), BF)
    else:
        n_y, n_x, size = split_rows
        out = pl.BlockSpec((n_x, n_y * size, tile), lambda j: (0, 0, j))
        shape = jax.ShapeDtypeStruct((n_x, n_y * size, feats), BF)
    return weight, out, shape


def down_first(pieces, plan, down_w, feats, rows, split_rows):
    hidden = down_w.shape[0]
    tile = column_tile(feats)
    anywhere = pl.BlockSpec(memory_space=pl.ANY)
    weight, out, shape = down_specs(rows, hidden, tile, feats, 0, split_rows)
    return pl.pallas_call(
        functools.partial(down_kernel, plan, len(pieces), split_rows),
        grid=(feats // tile,),
        in_specs=[anywhere] * len(pieces) + [weight],
        out_specs=[out, anywhere],
        out_shape=[shape, jax.ShapeDtypeStruct((rows, hidden), BF)],
        scratch_shapes=[
            pltpu.VMEM((rows, hidden), BF),
            pltpu.SemaphoreType.DMA((len(plan),)),
            pltpu.SemaphoreType.DMA,
        ],
        compiler_params=params(),
        cost_estimate=cost(
            2 * rows * hidden * feats, 2 * hidden * feats + 4 * rows * hidden
        ),
    )(*pieces, down_w)


def down_next(hidden_all, down_w, start, feats, split_rows):
    rows, hidden = hidden_all.shape
    tile = column_tile(feats)
    weight, out, shape = down_specs(rows, hidden, tile, feats, start // tile, split_rows)
    return pl.pallas_call(
        functools.partial(down_next_kernel, split_rows),
        grid=(feats // tile,),
        in_specs=[whole((rows, hidden)), weight],
        out_specs=out,
        out_shape=shape,
        compiler_params=params(),
        cost_estimate=cost(
            2 * rows * hidden * feats, 2 * hidden * feats + 2 * rows * hidden
        ),
    )(hidden_all, down_w)


def down_grad_kernel(hid, cot, out):
    out[...] = dot32(hid[...], cot[...], ((0,), (0,))).astype(BF)


def down_grad(hidden_all, cot_rows, feats):
    rows, hidden = hidden_all.shape
    tile = 512
    return pl.pallas_call(
        down_grad_kernel,
        grid=(hidden // tile,),
        in_specs=[
            pl.BlockSpec((rows, tile), lambda j: (0, j)),
            pl.BlockSpec((rows, feats), lambda j: (0, 0)),
        ],
        out_specs=pl.BlockSpec((tile, feats), lambda j: (j, 0)),
        out_shape=jax.ShapeDtypeStruct((hidden, feats), BF),
        compiler_params=pltpu.CompilerParams(vmem_limit_bytes=VMEM),
        cost_estimate=pl.CostEstimate(
            flops=2 * rows * hidden * feats,
            bytes_accessed=2 * hidden * feats + 2 * rows * hidden,
            transcendentals=0,
        ),
    )(hidden_all, cot_rows)


def row_stats_kernel(x, split, weight, out):
    n_z, rows, cols = x.shape
    total = jnp.zeros((rows, LANES), F32)
    raw = jnp.zeros((rows, LANES), F32)
    for z in range(n_z):
        raw = raw + dot32(x[z], split[z], ((1,), (1,)))
        for k in range(cols // LANES):
            at = slice(k * LANES, (k + 1) * LANES)
            part = x[z, :, at].astype(F32)
            total = total + part * part * weight[z, :, at]
    lane = lax.broadcasted_iota(jnp.int32, (rows, LANES), 1)
    out[...] = jnp.where(lane == LANES - 1, jnp.sum(total, axis=1, keepdims=True), raw)


def row_stats(x_got, split, weight):
    n_z, rows, cols = x_got.shape
    return pl.pallas_call(
        row_stats_kernel,
        out_shape=jax.ShapeDtypeStruct((rows, LANES), F32),
        compiler_params=pltpu.CompilerParams(vmem_limit_bytes=VMEM),
        cost_estimate=pl.CostEstimate(
            flops=2 * n_z * rows * cols * LANES,
            bytes_accessed=2 * n_z * cols * (rows + LANES),
            transcendentals=0,
        ),
    )(x_got, split, weight)


def hidden_grad_kernel(heads, cot, down_w, out):
    out[0] = dot32(cot[...], down_w[...], ((1,), (1,))).astype(BF)


def hidden_grad_part(heads, cot_rows, down_w, cols):
    rows, feats = cot_rows.shape[0], down_w.shape[1]
    tile = 512 if cols % 512 == 0 else cols
    steps = cols // tile
    n_heads = heads.shape[0]
    return pl.pallas_call(
        hidden_grad_kernel,
        grid_spec=pltpu.PrefetchScalarGridSpec(
            num_scalar_prefetch=1,
            grid=(n_heads, steps),
            in_specs=[
                pl.BlockSpec((rows, feats), lambda i, j, heads: (0, 0)),
                pl.BlockSpec((tile, feats), lambda i, j, heads: (heads[i] * steps + j, 0)),
            ],
            out_specs=pl.BlockSpec((1, rows, tile), lambda i, j, heads: (i, 0, j)),
        ),
        out_shape=jax.ShapeDtypeStruct((n_heads, rows, cols), BF),
        compiler_params=pltpu.CompilerParams(vmem_limit_bytes=VMEM),
        cost_estimate=pl.CostEstimate(
            flops=2 * rows * feats * cols * n_heads,
            bytes_accessed=2 * n_heads * cols * (feats + rows),
            transcendentals=0,
        ),
    )(heads, cot_rows, down_w)


def gather_plane(own):
    n_y, n_x, n_z = lax.axis_size("y"), lax.axis_size("x"), own.shape[0]
    rows, cols = own.shape[1:]
    if n_y != 2 or n_x != 2 or rows % 16:
        full = lax.all_gather(own, ("y", "x", "c"), axis=0, tiled=False)
        full = full.reshape(n_y, n_x, CORES, n_z, rows, cols).transpose(0, 1, 4, 3, 2, 5)
        full = full.reshape(n_y * n_x * rows, n_z * CORES * cols)
        return [full], [(0, None, 0, 0)], full
    half = n_z // 2
    side = shift(own, "x")
    over = shift(own, "y")
    corner_low = shift(over[:half], "x")
    corner_high = shift(side[half:], "y")
    found = [
        (own, 0, 0, 0),
        (side, 0, 1, 0),
        (over, 1, 0, 0),
        (corner_low, 1, 1, 0),
        (corner_high, 1, 1, half),
    ]
    pieces, plan = [], []
    for value, dy, dx, low in found:
        for dc, array in enumerate((value, shift(value, "c"))):
            for z in range(array.shape[0]):

                def row(dy=dy, dx=dx):
                    y = (lax.axis_index("y") + dy) % 2
                    x = (lax.axis_index("x") + dx) % 2
                    return (y * 2 + x) * rows

                def col(dc=dc, at=low + z):
                    c = (lax.axis_index("c") + dc) % CORES
                    return at * CORES * cols + c * cols

                plan.append((len(pieces), z, row, col))
            pieces.append(array)
    return pieces, plan, corner_low


def gather_heads(own, beside):
    rows, cols = own.shape
    if lax.axis_size("y") != 2:
        full = lax.all_gather(own, ("y", "c"), axis=1, tiled=True)
        return [full], [(0, None, 0, 0)], beside()
    over = shift(own, "y")
    mate = shift(own, "c")
    done = beside()
    over, *done = tie(over, *done)
    pieces, plan = [own, mate, over, shift(over, "c")], []
    for number in range(len(pieces)):

        def col(dy=number // 2, dc=number % 2):
            y = (lax.axis_index("y") + dy) % 2
            c = (lax.axis_index("c") + dc) % CORES
            return (y * CORES + c) * cols

        plan.append((number, None, 0, col))
    return pieces, plan, done


def gather_x(own):
    if lax.axis_size("x") != 2:
        return lax.all_gather(own, "x", axis=0, tiled=False)
    return jnp.stack(order(own, shift(own, "x"), lax.axis_index("x")))


def gather_table(own):
    if lax.axis_size("y") != 2:
        return lax.all_gather(own, ("y", "c"), axis=1, tiled=True)
    pair = jnp.concatenate(order(own, shift(own, "c"), lax.axis_index("c")), axis=1)
    return jnp.concatenate(order(pair, shift(pair, "y"), lax.axis_index("y")), axis=1)


def gather_stats(own):
    if lax.axis_size("y") != 2 or lax.axis_size("x") != 2:
        return lax.all_gather(lax.psum(own, "c"), ("y", "x"), axis=0, tiled=True)
    own = own + shift(own, "c")
    pair = jnp.concatenate(order(own, shift(own, "x"), lax.axis_index("x")))
    return jnp.concatenate(order(pair, shift(pair, "y"), lax.axis_index("y")))


def shards(
    attention,
    out_proj,
    residual,
    norm_gain,
    router,
    routes,
    cotangent,
    gate_weight,
    up_weight,
    down_weight,
):
    n_y, n_z, n_x = lax.axis_size("y"), lax.axis_size("z"), lax.axis_size("x")
    at_y, at_c = lax.axis_index("y"), lax.axis_index("c")
    at_z, at_x = lax.axis_index("z"), lax.axis_index("x")
    tok = attention.shape[0]
    cap = tok * 9 // 16
    parts = n_z // n_y
    feats = residual.shape[1]
    width = feats * n_y * CORES
    cols = width // (n_z * CORES)
    rows_total = n_z * n_x * cap
    swaps = [swap_pairs(n_y, n_z, n_x, parts, turn) for turn in range(parts)]
    gate_w, up_w, down_w = gate_weight[0], up_weight[0], down_weight[0]

    far_proj = shift(out_proj, "x") if n_x == 2 else None
    line = jnp.zeros((n_z * tok, attention.shape[1]), BF)
    arrived = [(shift(attention, "z", step), step) for step in range(1, n_z)]
    for block, step in [(attention, 0)] + arrived:
        at = (at_z + n_z - step) % n_z * tok
        line = lax.dynamic_update_slice(line, block, (at, 0))

    ids = jnp.arange(EXPERTS, dtype=jnp.int32)
    slot_ids = jnp.arange(cap, dtype=jnp.int32)
    pair = jnp.arange(tok * 2, dtype=jnp.int32)
    before = (pair[None, :] < pair[:, None]).astype(BF)

    def places(named):
        blocks = named.shape[0]
        hits = (named.reshape(blocks, tok * 2)[:, :, None] == ids).astype(BF)
        earlier = jnp.einsum("pq,bqe->bpe", before, hits, preferred_element_type=F32)
        slots = jnp.sum(earlier * hits.astype(F32), axis=2).astype(jnp.int32)
        slots = slots.reshape(blocks, tok, 2)
        either = None
        for k in range(2):
            same = named[:, None, None, :, k] == ids[None, :, None, None]
            same = same & (slots[:, None, None, :, k] == slot_ids[None, None, :, None])
            either = same if either is None else either | same
        return either.astype(BF)

    own_place = places(routes[None]).reshape(EXPERTS * cap, tok)

    both_ids = (routes[:, :1] + routes[:, 1:]).astype(BF)
    cot_wide = jnp.concatenate([cotangent, jnp.broadcast_to(both_ids, (tok, LANES))], axis=1)
    cot_send = dot32(own_place, cot_wide, ((1,), (0,))).astype(BF)
    cot_got = lax.all_to_all(
        cot_send.reshape(n_z, cap, feats + LANES), "z", split_axis=0, concat_axis=0, tiled=True
    )
    res_after, cot_got = tie(residual, cot_got)
    cot_rows = gather_x(cot_got).reshape(n_x, n_y, parts * cap, feats + LANES)
    cot_rows = cot_rows.transpose(1, 0, 2, 3).reshape(rows_total, feats + LANES)

    route_cols = jnp.pad(routes.astype(BF), ((0, 0), (0, LANES - 2)))
    res_cut = res_after.reshape(tok, parts, cols)
    res_got = [
        lax.ppermute(
            jnp.concatenate([pick(res_cut, (turn + at_z) % parts, 1), route_cols], axis=1),
            ALL_AXES,
            swaps[turn],
        )
        for turn in range(parts)
    ]
    if parts == 2:
        res_mid = jnp.stack(order(res_got[0], res_got[1], at_c))
    else:
        res_mid = res_got[0][None]
    mid_place = places(res_mid[:, :, cols : cols + 2].astype(jnp.int32))
    res_mid = res_mid[:, :, :cols].reshape(parts * tok, cols)
    table = jnp.concatenate([norm_gain.astype(F32)[None, :], router.T], axis=0)
    table = gather_table(table)
    gain_all = table[:1]
    gain_mid = lax.dynamic_slice(gain_all, (0, (at_z * CORES + at_c) * cols), (1, cols))
    own_table = pick(table.reshape(1 + EXPERTS, n_z, CORES, cols), at_c, 2)
    weight = 1.0 / (own_table[0] * own_table[0])
    weight = weight[:, None, :]
    high = lax.reduce_precision(own_table[1:], 8, 7)
    middle = lax.reduce_precision(own_table[1:] - high, 8, 7)
    low = own_table[1:] - high - middle
    split = jnp.concatenate([high, middle, low], axis=0).astype(BF).transpose(1, 0, 2)
    split = jnp.pad(split, ((0, 0), (0, LANES - split.shape[1]), (0, 0)))

    line, res_mid = tie(line, res_mid)
    if n_x == 2:
        near = dot32(line, out_proj, ((1,), (0,)))
        far = dot32(line, far_proj, ((1,), (0,)))
        keep, give = order(near, far, at_c ^ at_x)
    else:
        wide = lax.all_gather(out_proj, "x", axis=1, tiled=True)
        both = dot32(line, wide, ((1,), (0,))).reshape(-1, CORES, cols)
        keep, give = pick(both, at_c, 1), pick(both, 1 - at_c, 1)
    summed = keep + shift(give.astype(BF), "c").astype(F32)
    summed = summed.reshape(n_y, parts * tok, cols)
    proj_mid = pick(summed, at_y)
    for step in range(1, n_y):
        outgoing = pick(summed, (at_y + step) % n_y).astype(BF)
        proj_mid = proj_mid + shift(outgoing, "y", step).astype(F32)
    scaled = ((res_mid.astype(F32) + proj_mid) * gain_mid).astype(BF)

    x_send = jnp.einsum(
        "best,btd->ebsd",
        mid_place,
        scaled.reshape(parts, tok, cols),
        preferred_element_type=F32,
    ).astype(BF)
    x_send, cot_rows, split, weight = tie(x_send, cot_rows, split, weight)
    x_got = lax.all_to_all(
        x_send.reshape(n_z, parts * cap, cols), "z", split_axis=0, concat_axis=0, tiled=True
    )
    pieces, plan, _ = gather_plane(x_got)

    stats = gather_stats(row_stats(x_got, split, weight))

    back, x_got = tie(proj_mid.astype(BF), x_got)
    back = back.reshape(parts, tok, cols)
    got = [
        lax.ppermute(
            pick(back, (at_c + parts - turn) % parts), ALL_AXES, [(b, a) for a, b in swaps[turn]]
        )
        for turn in range(parts)
    ]
    if parts == 2:
        proj = jnp.concatenate(order(got[0], got[1], at_z % 2), axis=1)
    else:
        proj = got[0]
    stats, proj = tie(stats, proj)

    hidden_cols = gate_w.shape[1]
    near_heads = (at_y + 1 + jnp.arange(n_y, dtype=jnp.int32)) % n_y * CORES
    dh_give = hidden_grad_part(near_heads + 1 - at_c, cot_rows, down_w, hidden_cols)
    dh_got = shift(dh_give, "c")
    dh_keep = hidden_grad_part(near_heads + at_c, cot_rows, down_w, hidden_cols)
    hidden_grad = dh_keep[n_y - 1].astype(F32) + dh_got[n_y - 1].astype(F32)
    for step in range(1, n_y):
        outgoing = dh_keep[step - 1].astype(F32) + dh_got[step - 1].astype(F32)
        outgoing, stats, *pieces = tie(outgoing.astype(BF), stats, *pieces)
        hidden_grad = hidden_grad + shift(outgoing, "y", step).astype(F32)
    hidden_grad = hidden_grad.astype(BF)

    hidden_local, a_val, b_val, scale, x_rows = forward(
        pieces, plan, gate_w, up_w, stats, cot_rows, feats // LANES
    )
    hidden_local, hidden_grad = tie(hidden_local, hidden_grad)
    pieces, plan, (grad_gate, grad_up) = gather_heads(
        hidden_local, lambda: gate_up_grads(x_rows, a_val, b_val, hidden_grad, scale)
    )

    size = parts * cap
    split_rows = (n_y, n_x, size) if size % 16 == 0 else None
    half = feats // 2 if feats % 512 == 0 else feats
    outs = []
    for start in range(0, feats, half):
        if start == 0:
            partial_out, hidden_all = down_first(
                pieces, plan, down_w, half, rows_total, split_rows
            )
        else:
            partial_out = down_next(hidden_all, down_w, start, half, split_rows)
        if split_rows is None:
            partial_out = partial_out.reshape(n_y, n_x, size, half).transpose(1, 0, 2, 3)
            partial_out = partial_out.reshape(n_x, n_y * size, half)
        out_rows = pick(partial_out, at_x).astype(F32)
        for step in range(1, n_x):
            outgoing = pick(partial_out, (at_x + step) % n_x)
            out_rows = out_rows + shift(outgoing, "x", step).astype(F32)
        out_rows = out_rows.astype(BF).reshape(n_z, cap, half)
        if start == 0:
            out_rows, cot_late = tie(out_rows, cot_rows)
        outs.append(
            lax.all_to_all(out_rows, "z", split_axis=0, concat_axis=0, tiled=True)
        )
    returned = jnp.concatenate(outs, axis=2).reshape(EXPERTS * cap, feats)
    grad_down = down_grad(hidden_all, cot_late, feats)

    state = residual.astype(F32) + proj.astype(F32)
    layer_out = state + dot32(own_place, returned, ((0,), (0,)))
    return (layer_out, grad_gate[None], grad_up[None], grad_down[None])


def solution(mesh):
    heads, owners = mesh.shape["head"], mesh.shape["expert"]
    fine = Mesh(
        mesh.devices.reshape(heads // CORES, CORES, EXPERTS, owners // EXPERTS), ALL_AXES
    )
    head, expert = ("y", "c"), ("z", "x")
    return jax.shard_map(
        shards,
        mesh=fine,
        in_specs=(
            P(expert, head),
            P(head, expert),
            P(expert, head),
            P(head),
            P(head, None),
            P(expert, None),
            P(expert, head),
            P(expert, None, head),
            P(expert, None, head),
            P(expert, None, head),
        ),
        out_specs=(
            P(expert, head),
            P(expert, None, head),
            P(expert, None, head),
            P(expert, None, head),
        ),
        check_vma=False,
    )
```

```python
import functools

import jax
import jax.numpy as jnp
from jax import lax
from jax.experimental import pallas as pl
from jax.experimental.pallas import tpu as pltpu
from jax.sharding import Mesh, PartitionSpec as P

EPSILON = 1e-05
EXPERTS = 4
CORES = 2
LANES = 128
VMEM = 50 * 2**20
BF = jnp.bfloat16
F32 = jnp.float32
ALL_AXES = ("y", "c", "z", "x")


def shift(value, axis, step=1):
    size = lax.axis_size(axis)
    return lax.ppermute(value, axis, [(i, (i + step) % size) for i in range(size)])


def pick(stack, index, axis=0):
    return lax.dynamic_index_in_dim(stack, index, axis, keepdims=False)


def tie(*values):
    return lax.optimization_barrier(values)


def after(value, *others):
    return tie(value, *others)[0]


def swap_pairs(n_y, n_z, n_x, parts, turn):
    pairs = []
    for y in range(n_y):
        for c in range(CORES):
            for z in range(n_z):
                for x in range(n_x):
                    piece = (y * CORES + c) * parts + (turn + z) % parts
                    to_z, to_c = piece // CORES, piece % CORES
                    to_y = z // parts
                    source = ((y * CORES + c) * n_z + z) * n_x + x
                    target = ((to_y * CORES + to_c) * n_z + to_z) * n_x + x
                    pairs.append((source, target))
    return pairs


def dot32(a, b, dims):
    return lax.dot_general(a, b, (dims, ((), ())), preferred_element_type=F32)


def sigmoid(value):
    return 1.0 / (1.0 + jnp.exp(-value))


def order(mine, other, index):
    first = index == 0
    return jnp.where(first, mine, other), jnp.where(first, other, mine)


def place_copies(plan, refs, scratch, sems):
    copies = []
    for number, (ref, lead, row, col) in enumerate(plan):
        source = refs[ref] if lead is None else refs[ref].at[lead]
        n_rows, n_cols = source.shape
        row = pl.multiple_of(row(), 16) if callable(row) else row
        col = pl.multiple_of(col(), LANES) if callable(col) else col
        copies.append(
            pltpu.make_async_copy(
                source,
                scratch.at[pl.ds(row, n_rows), pl.ds(col, n_cols)],
                sems.at[number],
            )
        )
    return copies


def whole(shape):
    return pl.BlockSpec(shape, lambda *_: (0,) * len(shape))


def column_tile(cols):
    return 256 if cols % 256 == 0 else cols


def params():
    return pltpu.CompilerParams(vmem_limit_bytes=VMEM)


def cost(flops, bytes_accessed, transcendentals=0):
    return pl.CostEstimate(
        flops=flops, bytes_accessed=bytes_accessed, transcendentals=transcendentals
    )


def forward_kernel(plan, n_refs, width, *args):
    refs = args[:n_refs]
    gate_w, up_w, split, weight, hid, u_out, v_out, logits, x_out = args[n_refs:-4]
    x_all, inv, sems, sem = args[-4:]
    step = pl.program_id(0)
    rows = x_all.shape[0]
    keep = pltpu.make_async_copy(x_all, x_out, sem)

    @pl.when(step == 0)
    def _():
        copies = place_copies(plan, refs, x_all, sems)
        for copy in copies:
            copy.start()
        for copy in copies:
            copy.wait()
        keep.start()
        chunk = 48

        def squares(index, carry):
            at = pl.multiple_of(index * chunk, 16)
            total = jnp.zeros((chunk, LANES), F32)
            for k in range(width // LANES):
                part = x_all[pl.ds(at, chunk), k * LANES : (k + 1) * LANES].astype(F32)
                total = total + part * part * weight[:, k * LANES : (k + 1) * LANES]
            mean = jnp.sum(total, axis=1, keepdims=True) / width
            inv[pl.ds(at, chunk), :] = jnp.broadcast_to(
                lax.rsqrt(mean + EPSILON), (chunk, LANES)
            )
            return carry

        lax.fori_loop(0, rows // chunk, squares, 0)
        logits[...] = dot32(x_all[...], split[...], ((1,), (1,))) * inv[...]

    x = x_all[...]
    a = jnp.dot(x, gate_w[...], preferred_element_type=F32)
    b = jnp.dot(x, up_w[...], preferred_element_type=F32)
    inverse = inv[:, :1]
    a = a * inverse
    b = b * inverse
    s = sigmoid(a)
    act = a * s
    hid[...] = (act * b).astype(BF)
    u_out[...] = (b * (s + act * (1.0 - s)) * inverse).astype(BF)
    v_out[...] = (act * inverse).astype(BF)

    @pl.when(step == pl.num_programs(0) - 1)
    def _():
        keep.wait()


def forward(pieces, plan, rows, gate_w, up_w, split, weight):
    width, cols = gate_w.shape
    tile = 256 if cols % 256 == 0 else cols
    anywhere = pl.BlockSpec(memory_space=pl.ANY)
    return pl.pallas_call(
        functools.partial(forward_kernel, plan, len(pieces), width),
        grid=(cols // tile,),
        in_specs=[anywhere] * len(pieces)
        + [
            pl.BlockSpec((width, tile), lambda j: (0, j)),
            pl.BlockSpec((width, tile), lambda j: (0, j)),
            whole((LANES, width)),
            whole((1, width)),
        ],
        out_specs=[pl.BlockSpec((rows, tile), lambda j: (0, j))] * 3
        + [whole((rows, LANES)), anywhere],
        out_shape=[jax.ShapeDtypeStruct((rows, cols), BF)] * 3
        + [
            jax.ShapeDtypeStruct((rows, LANES), F32),
            jax.ShapeDtypeStruct((rows, width), BF),
        ],
        scratch_shapes=[
            pltpu.VMEM((rows, width), BF),
            pltpu.VMEM((rows, LANES), F32),
            pltpu.SemaphoreType.DMA((len(plan),)),
            pltpu.SemaphoreType.DMA,
        ],
        compiler_params=pltpu.CompilerParams(vmem_limit_bytes=VMEM),
        cost_estimate=cost(4 * rows * width * cols, 4 * width * cols + 2 * rows * width),
    )(*pieces, gate_w, up_w, split, weight)


def prob_kernel(logits, meta, prob):
    lane = lax.broadcasted_iota(jnp.int32, logits.shape, 1)
    own = lax.axis_index("z")
    other = meta[...].astype(F32).astype(jnp.int32) - own
    expert = lane % EXPERTS
    sign = (expert == own).astype(F32) - (expert == other).astype(F32)
    sign = jnp.where(lane < 3 * EXPERTS, sign, 0.0)
    gap = jnp.sum(logits[...] * sign, axis=1, keepdims=True)
    prob[...] = jnp.broadcast_to(sigmoid(gap), prob.shape)


def row_probs(logits, cot_rows, meta_block):
    rows = logits.shape[0]
    return pl.pallas_call(
        prob_kernel,
        grid=(1,),
        in_specs=[
            whole((rows, LANES)),
            pl.BlockSpec((rows, LANES), lambda j: (0, meta_block)),
        ],
        out_specs=whole((rows, LANES)),
        out_shape=jax.ShapeDtypeStruct((rows, LANES), F32),
        compiler_params=params(),
        cost_estimate=cost(20 * rows * LANES, 10 * rows * LANES, rows),
    )(logits, cot_rows)


def weight_grad_kernel(n_terms, *args):
    x, factor, prob = args[:3]
    terms = args[3 : 3 + n_terms]
    out, grad = args[3 + n_terms :]

    @pl.when(pl.program_id(0) == 0)
    def _():
        for k in range(factor.shape[1] // LANES):
            at = slice(k * LANES, (k + 1) * LANES)
            dh = terms[0][:, at].astype(F32)
            for term in terms[1:]:
                dh = dh + term[:, at].astype(F32)
            grad[:, at] = (dh * prob[...] * factor[:, at].astype(F32)).astype(BF)

    out[...] = dot32(x[...], grad[...], ((0,), (0,))).astype(BF)


def weight_grad(x_rows, factor, prob, stacks, terms):
    rows, width = x_rows.shape
    cols = factor.shape[1]
    tile = 512
    last = [
        pl.BlockSpec((pl.squeezed, rows, cols), lambda j, at=stack.shape[0] - 1: (at, 0, 0))
        for stack in stacks
    ]
    return pl.pallas_call(
        functools.partial(weight_grad_kernel, len(stacks) + len(terms)),
        grid=(width // tile,),
        in_specs=[
            pl.BlockSpec((rows, tile), lambda j: (0, j)),
            whole((rows, cols)),
            whole((rows, LANES)),
        ]
        + last
        + [whole((rows, cols))] * len(terms),
        out_specs=pl.BlockSpec((tile, cols), lambda j: (j, 0)),
        out_shape=jax.ShapeDtypeStruct((width, cols), BF),
        scratch_shapes=[pltpu.VMEM((rows, cols), BF)],
        compiler_params=params(),
        cost_estimate=cost(
            2 * rows * width * cols, 2 * width * cols + 2 * rows * width + 8 * rows * cols
        ),
    )(x_rows, factor, prob, *stacks, *terms)


def down_store(value, out, split_rows):
    if split_rows is None:
        out[...] = value
        return
    n_y, n_x, size = split_rows
    for y in range(n_y):
        for x in range(n_x):
            at = (y * n_x + x) * size
            out[x, y * size : (y + 1) * size, :] = value[at : at + size]


def down_kernel(plan, n_refs, split_rows, *args):
    refs = args[:n_refs]
    down_w, prob, out, hid_out, hid, sems, sem = args[n_refs:]
    step = pl.program_id(0)
    keep = pltpu.make_async_copy(hid, hid_out, sem)

    @pl.when(step == 0)
    def _():
        copies = place_copies(plan, refs, hid, sems)
        for copy in copies:
            copy.start()
        for copy in copies:
            copy.wait()
        keep.start()

    value = jnp.dot(hid[...], down_w[...], preferred_element_type=F32) * prob[:, :1]
    down_store(value.astype(BF), out, split_rows)

    @pl.when(step == pl.num_programs(0) - 1)
    def _():
        keep.wait()


def down_next_kernel(split_rows, hid, down_w, prob, out):
    value = jnp.dot(hid[...], down_w[...], preferred_element_type=F32) * prob[:, :1]
    down_store(value.astype(BF), out, split_rows)


def down_specs(rows, hidden, tile, feats, base, split_rows):
    weight = pl.BlockSpec((hidden, tile), lambda j: (0, j + base))
    if split_rows is None:
        out = pl.BlockSpec((rows, tile), lambda j: (0, j))
        shape = jax.ShapeDtypeStruct((rows, feats), BF)
    else:
        n_y, n_x, size = split_rows
        out = pl.BlockSpec((n_x, n_y * size, tile), lambda j: (0, 0, j))
        shape = jax.ShapeDtypeStruct((n_x, n_y * size, feats), BF)
    return weight, out, shape


def down_first(pieces, plan, down_w, prob, feats, split_rows):
    hidden, rows = down_w.shape[0], prob.shape[0]
    tile = column_tile(feats)
    anywhere = pl.BlockSpec(memory_space=pl.ANY)
    weight, out, shape = down_specs(rows, hidden, tile, feats, 0, split_rows)
    return pl.pallas_call(
        functools.partial(down_kernel, plan, len(pieces), split_rows),
        grid=(feats // tile,),
        in_specs=[anywhere] * len(pieces) + [weight, whole((rows, LANES))],
        out_specs=[out, anywhere],
        out_shape=[shape, jax.ShapeDtypeStruct((rows, hidden), BF)],
        scratch_shapes=[
            pltpu.VMEM((rows, hidden), BF),
            pltpu.SemaphoreType.DMA((len(plan),)),
            pltpu.SemaphoreType.DMA,
        ],
        compiler_params=params(),
        cost_estimate=cost(
            2 * rows * hidden * feats, 2 * hidden * feats + 4 * rows * hidden
        ),
    )(*pieces, down_w, prob)


def down_next(hidden_all, down_w, prob, start, feats, split_rows):
    rows, hidden = hidden_all.shape
    tile = column_tile(feats)
    weight, out, shape = down_specs(rows, hidden, tile, feats, start // tile, split_rows)
    return pl.pallas_call(
        functools.partial(down_next_kernel, split_rows),
        grid=(feats // tile,),
        in_specs=[whole((rows, hidden)), weight, whole((rows, LANES))],
        out_specs=out,
        out_shape=shape,
        compiler_params=params(),
        cost_estimate=cost(
            2 * rows * hidden * feats, 2 * hidden * feats + 2 * rows * hidden
        ),
    )(hidden_all, down_w, prob)


def down_grad_kernel(n_pieces, steps, *args):
    pieces = args[1 : 1 + n_pieces]
    cot, prob, out, scaled = args[1 + n_pieces], args[2 + n_pieces], args[-2], args[-1]
    step = pl.program_id(0)

    @pl.when(step == 0)
    def _():
        for k in range(scaled.shape[1] // LANES):
            at = slice(k * LANES, (k + 1) * LANES)
            scaled[:, at] = (cot[:, at].astype(F32) * prob[...]).astype(BF)

    for number in range(n_pieces):

        @pl.when(step // steps == number)
        def _(piece=pieces[number]):
            out[...] = dot32(piece[...], scaled[...], ((0,), (0,))).astype(BF)


def down_grad(heads, pieces, cot_rows, prob, feats):
    rows, cols = pieces[0].shape
    tile = 512 if cols % 512 == 0 else cols
    steps = cols // tile
    n_pieces = len(pieces)

    def piece_spec(number):
        return pl.BlockSpec(
            (rows, tile), lambda i, heads: (0, jnp.clip(i - number * steps, 0, steps - 1))
        )

    return pl.pallas_call(
        functools.partial(down_grad_kernel, n_pieces, steps),
        grid_spec=pltpu.PrefetchScalarGridSpec(
            num_scalar_prefetch=1,
            grid=(n_pieces * steps,),
            in_specs=[piece_spec(number) for number in range(n_pieces)]
            + [pl.BlockSpec((rows, feats), lambda i, heads: (0, 0)), whole((rows, LANES))],
            out_specs=pl.BlockSpec(
                (tile, feats), lambda i, heads: (heads[i // steps] * steps + i % steps, 0)
            ),
            scratch_shapes=[pltpu.VMEM((rows, feats), BF)],
        ),
        out_shape=jax.ShapeDtypeStruct((n_pieces * cols, feats), BF),
        compiler_params=params(),
        cost_estimate=cost(
            2 * rows * n_pieces * cols * feats, 2 * n_pieces * cols * (feats + rows)
        ),
    )(heads, *pieces, cot_rows, prob)


def hidden_grad_kernel(n_heads, heads, cot, down_w, give, keep):
    value = dot32(cot[...], down_w[...], ((1,), (1,))).astype(BF)

    @pl.when(pl.program_id(0) < n_heads)
    def _():
        give[...] = value

    @pl.when(pl.program_id(0) >= n_heads)
    def _():
        keep[...] = value


def hidden_grad_parts(heads, cot_rows, down_w, cols):
    rows, feats = cot_rows.shape[0], down_w.shape[1]
    tile = 512 if cols % 512 == 0 else cols
    steps = cols // tile
    n_heads = heads.shape[0] // 2

    def give_at(i, j, heads):
        first = i < n_heads
        return jnp.where(first, i, n_heads - 1), 0, jnp.where(first, j, steps - 1)

    def keep_at(i, j, heads):
        first = i < n_heads
        return jnp.where(first, 0, i - n_heads), 0, jnp.where(first, 0, j)

    block = (pl.squeezed, rows, tile)
    return pl.pallas_call(
        functools.partial(hidden_grad_kernel, n_heads),
        grid_spec=pltpu.PrefetchScalarGridSpec(
            num_scalar_prefetch=1,
            grid=(2 * n_heads, steps),
            in_specs=[
                pl.BlockSpec((rows, feats), lambda i, j, heads: (0, 0)),
                pl.BlockSpec((tile, feats), lambda i, j, heads: (heads[i] * steps + j, 0)),
            ],
            out_specs=[pl.BlockSpec(block, give_at), pl.BlockSpec(block, keep_at)],
        ),
        out_shape=[jax.ShapeDtypeStruct((n_heads, rows, cols), BF)] * 2,
        compiler_params=params(),
        cost_estimate=cost(
            4 * rows * feats * cols * n_heads, 4 * n_heads * cols * (feats + rows)
        ),
    )(heads, cot_rows, down_w)


def gather_plane(own):
    n_y, n_x, n_z = lax.axis_size("y"), lax.axis_size("x"), own.shape[0]
    rows, cols = own.shape[1:]
    if n_y != 2 or n_x != 2 or rows % 16:
        full = lax.all_gather(own, ("y", "x", "c"), axis=0, tiled=False)
        full = full.reshape(n_y, n_x, CORES, n_z, rows, cols).transpose(0, 1, 4, 3, 2, 5)
        full = full.reshape(n_y * n_x * rows, n_z * CORES * cols)
        return [full], [(0, None, 0, 0)], full
    half = n_z // 2
    side = shift(own, "x")
    over = shift(own, "y")
    corner_low = shift(over[:half], "x")
    corner_high = shift(side[half:], "y")
    found = [
        (own, 0, 0, 0),
        (side, 0, 1, 0),
        (over, 1, 0, 0),
        (corner_low, 1, 1, 0),
        (corner_high, 1, 1, half),
    ]
    pieces, plan = [], []
    for value, dy, dx, low in found:
        for dc, array in enumerate((value, shift(value, "c"))):
            for z in range(array.shape[0]):

                def row(dy=dy, dx=dx):
                    y = (lax.axis_index("y") + dy) % 2
                    x = (lax.axis_index("x") + dx) % 2
                    return (y * 2 + x) * rows

                def col(dc=dc, at=low + z):
                    c = (lax.axis_index("c") + dc) % CORES
                    return at * CORES * cols + c * cols

                plan.append((len(pieces), z, row, col))
            pieces.append(array)
    return pieces, plan, corner_low


def gather_heads(own, beside):
    rows, cols = own.shape
    if lax.axis_size("y") != 2:
        full = lax.all_gather(own, ("y", "c"), axis=1, tiled=True)
        return [full], [(0, None, 0, 0)], beside(own)
    over = shift(own, "y")
    mate = shift(own, "c")
    done = beside(mate)
    over = after(over, done[-1])
    pieces, plan = [own, mate, over, shift(over, "c")], []
    for number in range(len(pieces)):

        def col(dy=number // 2, dc=number % 2):
            y = (lax.axis_index("y") + dy) % 2
            c = (lax.axis_index("c") + dc) % CORES
            return (y * CORES + c) * cols

        plan.append((number, None, 0, col))
    return pieces, plan, done


def gather_x(own):
    if lax.axis_size("x") != 2:
        return lax.all_gather(own, "x", axis=0, tiled=False)
    return jnp.stack(order(own, shift(own, "x"), lax.axis_index("x")))


def gather_table(own):
    if lax.axis_size("y") != 2:
        return lax.all_gather(own, ("y", "c"), axis=1, tiled=True)
    pair = jnp.concatenate(order(own, shift(own, "c"), lax.axis_index("c")), axis=1)
    return jnp.concatenate(order(pair, shift(pair, "y"), lax.axis_index("y")), axis=1)


def shards(
    attention,
    out_proj,
    residual,
    norm_gain,
    router,
    routes,
    cotangent,
    gate_weight,
    up_weight,
    down_weight,
):
    n_y, n_z, n_x = lax.axis_size("y"), lax.axis_size("z"), lax.axis_size("x")
    at_y, at_c = lax.axis_index("y"), lax.axis_index("c")
    at_z, at_x = lax.axis_index("z"), lax.axis_index("x")
    tok = attention.shape[0]
    cap = tok * 9 // 16
    parts = n_z // n_y
    feats = residual.shape[1]
    width = feats * n_y * CORES
    cols = width // (n_z * CORES)
    rows_total = n_z * n_x * cap
    swaps = [swap_pairs(n_y, n_z, n_x, parts, turn) for turn in range(parts)]
    gate_w, up_w, down_w = gate_weight[0], up_weight[0], down_weight[0]

    far_proj = shift(out_proj, "x") if n_x == 2 else None
    line = jnp.zeros((n_z * tok, attention.shape[1]), BF)
    arrived = [(shift(attention, "z", step), step) for step in range(1, n_z)]
    for block, step in [(attention, 0)] + arrived:
        at = (at_z + n_z - step) % n_z * tok
        line = lax.dynamic_update_slice(line, block, (at, 0))

    ids = jnp.arange(EXPERTS, dtype=jnp.int32)
    slot_ids = jnp.arange(cap, dtype=jnp.int32)
    pair = jnp.arange(tok * 2, dtype=jnp.int32)
    before = (pair[None, :] < pair[:, None]).astype(BF)

    def places(named):
        blocks = named.shape[0]
        hits = (named.reshape(blocks, tok * 2)[:, :, None] == ids).astype(BF)
        earlier = jnp.einsum("pq,bqe->bpe", before, hits, preferred_element_type=F32)
        slots = jnp.sum(earlier * hits.astype(F32), axis=2).astype(jnp.int32)
        slots = slots.reshape(blocks, tok, 2)
        either = None
        for k in range(2):
            same = named[:, None, None, :, k] == ids[None, :, None, None]
            same = same & (slots[:, None, None, :, k] == slot_ids[None, None, :, None])
            either = same if either is None else either | same
        return either.astype(BF)

    own_place = places(routes[None]).reshape(EXPERTS * cap, tok)

    route_cols = jnp.pad(routes.astype(BF), ((0, 0), (0, LANES - 2)))
    res_cut = residual.reshape(tok, parts, cols)
    res_got = [
        lax.ppermute(
            jnp.concatenate([pick(res_cut, (turn + at_z) % parts, 1), route_cols], axis=1),
            ALL_AXES,
            swaps[turn],
        )
        for turn in range(parts)
    ]
    if parts == 2:
        res_mid = jnp.stack(order(res_got[0], res_got[1], at_c))
    else:
        res_mid = res_got[0][None]
    mid_place = places(res_mid[:, :, cols : cols + 2].astype(jnp.int32))
    res_mid = res_mid[:, :, :cols].reshape(parts * tok, cols)
    table = jnp.concatenate([norm_gain.astype(F32)[None, :], router.T], axis=0)
    table = gather_table(table)
    gain_all = table[:1]
    gain_mid = lax.dynamic_slice(gain_all, (0, (at_z * CORES + at_c) * cols), (1, cols))
    weight = 1.0 / (gain_all * gain_all)
    high = lax.reduce_precision(table[1:], 8, 7)
    middle = lax.reduce_precision(table[1:] - high, 8, 7)
    low = table[1:] - high - middle
    split = jnp.concatenate([high, middle, low], axis=0).astype(BF)
    split = jnp.pad(split, ((0, LANES - split.shape[0]), (0, 0)))

    if n_x == 2:
        near = dot32(line, out_proj, ((1,), (0,)))
        far = dot32(line, far_proj, ((1,), (0,)))
        keep, give = order(near, far, at_c ^ at_x)
    else:
        wide = lax.all_gather(out_proj, "x", axis=1, tiled=True)
        both = dot32(line, wide, ((1,), (0,))).reshape(-1, CORES, cols)
        keep, give = pick(both, at_c, 1), pick(both, 1 - at_c, 1)
    summed = keep + shift(give.astype(BF), "c").astype(F32)
    summed = summed.reshape(n_y, parts * tok, cols)
    proj_mid = pick(summed, at_y)
    for step in range(1, n_y):
        outgoing = pick(summed, (at_y + step) % n_y).astype(BF)
        proj_mid = proj_mid + shift(outgoing, "y", step).astype(F32)
    scaled = ((res_mid.astype(F32) + proj_mid) * gain_mid).astype(BF)

    x_send = jnp.einsum(
        "best,btd->ebsd",
        mid_place,
        scaled.reshape(parts, tok, cols),
        preferred_element_type=F32,
    ).astype(BF)
    x_got = lax.all_to_all(
        x_send.reshape(n_z, parts * cap, cols), "z", split_axis=0, concat_axis=0, tiled=True
    )

    back = after(proj_mid.astype(BF), x_got)
    back = back.reshape(parts, tok, cols)
    got = [
        lax.ppermute(
            pick(back, (at_c + parts - turn) % parts), ALL_AXES, [(b, a) for a, b in swaps[turn]]
        )
        for turn in range(parts)
    ]
    if parts == 2:
        proj = jnp.concatenate(order(got[0], got[1], at_z % 2), axis=1)
    else:
        proj = got[0]

    pieces, plan, corner = gather_plane(x_got)
    pieces[0], proj = tie(pieces[0], proj)

    both_ids = (routes[:, :1] + routes[:, 1:]).astype(BF)
    cot_wide = jnp.concatenate([cotangent, jnp.broadcast_to(both_ids, (tok, LANES))], axis=1)
    cot_send = dot32(own_place, cot_wide, ((1,), (0,))).astype(BF)
    cot_send = after(cot_send, x_got)
    cot_got = lax.all_to_all(
        cot_send.reshape(n_z, cap, feats + LANES), "z", split_axis=0, concat_axis=0, tiled=True
    )
    cot_got = after(cot_got, corner, *pieces[-2:])
    cot_rows = gather_x(cot_got).reshape(n_x, n_y, parts * cap, feats + LANES)
    cot_rows = cot_rows.transpose(1, 0, 2, 3).reshape(rows_total, feats + LANES)

    hidden_cols = gate_w.shape[1]
    hidden_local, u_val, v_val, logits, x_rows = forward(
        pieces, plan, rows_total, gate_w, up_w, split, weight
    )

    prob = row_probs(logits, cot_rows, feats // LANES)
    near_heads = (at_y + 1 + jnp.arange(n_y, dtype=jnp.int32)) % n_y * CORES

    heads = jnp.concatenate([near_heads + 1 - at_c, near_heads + at_c])

    def beside(mate):
        return hidden_grad_parts(heads, after(cot_rows, mate), down_w, hidden_cols)

    pieces, plan, (dh_give, dh_keep) = gather_heads(hidden_local, beside)
    dh_got = shift(dh_give, "c")
    going = [
        (dh_keep[step - 1].astype(F32) + dh_got[step - 1].astype(F32)).astype(BF)
        for step in range(1, n_y)
    ]

    size = parts * cap
    split_rows = (n_y, n_x, size) if size % 16 == 0 else None
    half = feats // 2 if feats % 512 == 0 else feats
    outs, sums = [], []
    for start in range(0, feats, half):
        if start == 0:
            partial_out, hidden_all = down_first(
                pieces, plan, down_w, prob, half, split_rows
            )
        else:
            hidden_all = after(hidden_all, *going)
            partial_out = down_next(hidden_all, down_w, prob, start, half, split_rows)
        if split_rows is None:
            partial_out = partial_out.reshape(n_y, n_x, size, half).transpose(1, 0, 2, 3)
            partial_out = partial_out.reshape(n_x, n_y * size, half)
        out_rows = pick(partial_out, at_x).astype(F32)
        for step in range(1, n_x):
            outgoing = pick(partial_out, (at_x + step) % n_x)
            out_rows = out_rows + shift(outgoing, "x", step).astype(F32)
        out_rows = out_rows.astype(BF).reshape(n_z, cap, half)
        sums.append(out_rows)
        outs.append(
            lax.all_to_all(out_rows, "z", split_axis=0, concat_axis=0, tiled=True)
        )
    dh_terms = [shift(value, "y", step + 1) for step, value in enumerate(going)]
    returned = jnp.concatenate(outs, axis=2).reshape(EXPERTS * cap, feats)
    heads = jnp.zeros((1,), jnp.int32)
    cot_late = cot_rows
    grad_down = down_grad(heads, [hidden_all], cot_late, prob, feats)
    parts_of = (dh_keep, dh_got), [after(term, sums[0]) for term in dh_terms]
    grad_gate = weight_grad(x_rows, u_val, prob, *parts_of)
    parts_of = (dh_keep, dh_got), [after(term, sums[-1]) for term in dh_terms]
    grad_up = weight_grad(x_rows, v_val, prob, *parts_of)

    state = residual.astype(F32) + proj.astype(F32)
    layer_out = state + dot32(own_place, returned, ((0,), (0,)))
    return (layer_out, grad_gate[None], grad_up[None], grad_down[None])


def solution(mesh):
    heads, owners = mesh.shape["head"], mesh.shape["expert"]
    fine = Mesh(
        mesh.devices.reshape(heads // CORES, CORES, EXPERTS, owners // EXPERTS), ALL_AXES
    )
    head, expert = ("y", "c"), ("z", "x")
    return jax.shard_map(
        shards,
        mesh=fine,
        in_specs=(
            P(expert, head),
            P(head, expert),
            P(expert, head),
            P(head),
            P(head, None),
            P(expert, None),
            P(expert, head),
            P(expert, None, head),
            P(expert, None, head),
            P(expert, None, head),
        ),
        out_specs=(
            P(expert, head),
            P(expert, None, head),
            P(expert, None, head),
            P(expert, None, head),
        ),
        check_vma=False,
    )
```
